32 devices in a mesh: grp: 2 (over y), seq: 4 (over z), head: 2 (over x), rep: 2 (over core).
Axes of the slice: x: 2, y: 2, z: 4, core: 2. Of those that a mesh axis runs over, the one named last changes fastest.
Arguments:
- activations: bfloat16 [16384, 4096], P(('grp', 'seq', 'rep'), 'head'), parts along dimension 0, may hold values from -6 to 6
- cotangent: bfloat16 [16384, 4096], P(('grp', 'seq', 'rep'), 'head'), parts along dimension 0, may hold values from -6 to 6
- b_proj: bfloat16 [16384, 128], P(('grp', 'seq', 'rep')), parts along dimension 0, may hold values from -6 to 6
- c_proj: bfloat16 [16384, 128], P(('grp', 'seq', 'rep')), parts along dimension 0, may hold values from -0.5 to 0.5
- dt_raw: float32 [32, 16384], P('head', ('grp', 'seq', 'rep')), parts along dimension 1, may hold values from -5.2 to -3.8
- resets: int32 [16384], P(('grp', 'seq', 'rep')), parts along dimension 0, may hold values 0 or 1
- agents: int32 [16384], P(('grp', 'seq', 'rep')), parts along dimension 0, may hold values from 0 to 63
- agent_bias: float32 [32, 64], P('head'), may hold values from -0.7 to 0.7
- a_log: float32 [32], P('head'), may hold values from -9.5 to 1.5
- d_skip: float32 [32], P('head'), may hold values from 0.5 to 2
Outputs:
- grad_input: bfloat16 [16384, 4096], P(('grp', 'seq', 'rep'), 'head'), parts along dimension 0
- grad_b: float32 [16384, 128], P(('grp', 'seq', 'rep')), parts along dimension 0
- grad_c: float32 [16384, 128], P(('grp', 'seq', 'rep')), parts along dimension 0
- grad_rate: float32 [32, 16384], P('head', ('grp', 'seq', 'rep')), parts along dimension 1
The draws below stay inside these ranges and needn't reach their ends.
There are 2 independent parts, one for each index of `grp`. The reference program is written for one: setup_inputs(seed, part) draws one part's arguments, and reference() takes and returns one part's arrays. A program takes and returns all parts, laid end to end along the dimension named above; an argument that names none is the same for every part. Nothing has to cross between parts.
All inputs are finite; a program needn't handle non-finite values. No bound on the sum of `resets` on one device may be relied on, other than what follows from the above.
Results may differ from the reference program's by a relative error of at most 0.01.
Values sent between devices are 32-bit elements; how exact they have to be, the bound alone decides.
A program may use at most 256 MiB of HBM per device.

```python
from functools import partial
import jax
import jax.numpy as jnp
from jax import lax

HEADS = 32
HEAD_DIM = 128
STATE = 128
AGENTS = 64
BLOCK = 256
TOKENS = 8192


def draw_a_log(key, part):
    slow_share = 0.5
    slow_heads = jax.random.uniform(jax.random.fold_in(key, 1), (HEADS,), jnp.float32) < slow_share
    slow_value = jax.random.uniform(jax.random.fold_in(key, 2), (HEADS,), jnp.float32, -9.5, -8.0)
    fast_value = jax.random.uniform(jax.random.fold_in(key, 3), (HEADS,), jnp.float32, 0.5, 1.5)
    return jnp.where(slow_heads, slow_value, fast_value)


def with_ends(values, stream_key, least, largest):
    longest = values.shape.index(max(values.shape))
    spots = []
    for shift in (0, 1):
        where = [jax.random.randint(jax.random.fold_in(stream_key, axis), (), 0, length) for axis, length in enumerate(values.shape)]
        where[longest] = (where[longest] + shift) % values.shape[longest]
        spots.append(tuple(where))
    return values.at[spots[0]].set(least).at[spots[1]].set(largest)


def levels(rng, shape, shards, low, top_value):
    level, own = 1.0, jax.random.fold_in(rng, 6)
    for dim, parts in shards:
        draws = jnp.exp(jax.random.uniform(jax.random.fold_in(own, dim), (parts,), jnp.float32, low / len(shards), top_value / len(shards)))
        level = level * jnp.repeat(draws, shape[dim] // parts).reshape([-1 if axis == dim else 1 for axis in range(len(shape))])
    return level


def gaussian(rng, dims, scale, bound, split=(), dtype=jnp.bfloat16):
    drawn = scale * jax.random.normal(rng, dims, jnp.float32)
    if split:
        drawn = drawn * levels(rng, dims, split, -0.22, 0.18)
    return jnp.clip(drawn, -bound, bound).astype(dtype)


def setup_inputs(seed: int = 0, part: int = 0) -> dict:
    arg_keys = jax.random.split(jax.random.key(seed), 11)
    part_splits = jax.random.split(jax.random.fold_in(arg_keys[10], part), 11)
    return {
        "activations": gaussian(part_splits[0], (TOKENS, HEADS * HEAD_DIM), 1.0, 6.0, ((0, 8), (1, 2))),
        "cotangent": gaussian(part_splits[1], (TOKENS, HEADS * HEAD_DIM), 1.0, 6.0, ((0, 8), (1, 2))),
        "b_proj": gaussian(part_splits[2], (TOKENS, STATE), 1.0, 6.0, ((0, 8),)),
        "c_proj": gaussian(part_splits[3], (TOKENS, STATE), STATE ** -0.5, 0.5, ((0, 8),)),
        "dt_raw": jnp.clip(-5.2 + 1.3999999 * jax.random.uniform(part_splits[4], (HEADS, TOKENS), jnp.float32) ** levels(part_splits[4], (HEADS, TOKENS), ((0, 2), (1, 8)), -0.2, 0.2), -5.2, -3.8),
        "resets": with_ends((jax.random.randint(part_splits[5], (TOKENS,), 0, 4096) < 1).astype(jnp.int32), jax.random.fold_in(part_splits[5], 1), 0, 1),
        "agents": with_ends(jax.random.randint(part_splits[6], (TOKENS,), 0, AGENTS), jax.random.fold_in(part_splits[6], 1), 0, AGENTS - 1).astype(jnp.int32),
        "agent_bias": jnp.clip(jax.random.uniform(arg_keys[7], (HEADS, AGENTS), jnp.float32, -0.7, 0.7) * levels(arg_keys[7], (HEADS, AGENTS), ((0, 2),), -0.4, 0.0), -0.7, 0.7),
        "a_log": draw_a_log(jax.random.fold_in(arg_keys[10], 71), part),
        "d_skip": jnp.clip(0.5 + 1.5 * jax.random.uniform(arg_keys[9], (HEADS,), jnp.float32) ** levels(arg_keys[9], (HEADS,), ((0, 2),), -0.2, 0.2), 0.5, 2.0),
    }


def block_terms(carried, pieces, rate, d_skip):
    x_blk, b_blk, c_blk, raw_blk, bias_blk, reset_blk = pieces
    head_count = carried.shape[0]
    head_width = carried.shape[1]
    length = x_blk.shape[0]
    x_heads = x_blk.reshape(length, head_count, head_width)
    step_size = jax.nn.softplus(raw_blk + bias_blk)
    log_decay = -rate[:, None] * step_size
    cumulative = jnp.cumsum(log_decay, axis=1)
    episode = jnp.cumsum(reset_blk.astype(jnp.int32))
    position = jnp.arange(length)
    causal = (position[:, None] >= position[None, :]) & (episode[:, None] == episode[None, :])
    log_gap = cumulative[:, :, None] - cumulative[:, None, :]
    within = jnp.where(causal[None], jnp.exp(jnp.where(causal[None], log_gap, 0.0)), 0.0)
    scores = jnp.dot(c_blk, b_blk.T, precision=lax.Precision.HIGHEST, preferred_element_type=jnp.float32)
    mixing = (scores[None] * within * step_size[:, None, :]).astype(jnp.bfloat16)
    intra_part = jnp.einsum('hij,jhp->ihp', mixing, x_heads, preferred_element_type=jnp.float32)
    entry_decay = jnp.exp(cumulative) * (episode == 0).astype(jnp.float32)[None, :]
    c_scaled = (entry_decay[:, :, None] * c_blk[None]).astype(jnp.bfloat16)
    inter_part = jnp.einsum('hin,hpn->ihp', c_scaled, carried.astype(jnp.bfloat16), preferred_element_type=jnp.float32)
    skip_part = d_skip[None, :, None] * x_heads.astype(jnp.float32)
    output = (intra_part + inter_part + skip_part).reshape(length, head_count * head_width).astype(jnp.bfloat16)
    same_end = (episode == episode[-1]).astype(jnp.float32)[None, :]
    to_end = jnp.exp(cumulative[:, -1:] - cumulative) * same_end * step_size
    b_scaled = (to_end[:, :, None] * b_blk[None]).astype(jnp.bfloat16)
    added_state = jnp.einsum('jhp,hjn->hpn', x_heads, b_scaled, preferred_element_type=jnp.float32)
    carry_decay = jnp.exp(cumulative[:, -1]) * (episode[-1] == 0).astype(jnp.float32)
    next_state = carry_decay[:, None, None] * carried + added_state
    return (next_state, output)

def run_blocks(activations, b_full, c_full, raw_rates, bias_rates, resets, rate, d_skip, carried):
    token_count = activations.shape[0]
    head_count = raw_rates.shape[0]
    block_count = token_count // BLOCK
    pieces = (activations.reshape(block_count, BLOCK, -1), b_full.reshape(block_count, BLOCK, -1), c_full.reshape(block_count, BLOCK, -1), raw_rates.reshape(head_count, block_count, BLOCK).transpose(1, 0, 2), bias_rates.reshape(head_count, block_count, BLOCK).transpose(1, 0, 2), resets.reshape(block_count, BLOCK))
    final_state, block_outputs = lax.scan(partial(block_terms, rate=rate, d_skip=d_skip), carried, pieces)
    return (block_outputs.reshape(token_count, -1), final_state)

def reference(activations, cotangent, b_proj, c_proj, dt_raw, resets, agents, agent_bias, a_log, d_skip):
    bias_rates = jnp.take(agent_bias, agents.astype(jnp.int32), axis=1)
    rate = jnp.exp(a_log)
    start_state = jnp.zeros((HEADS, HEAD_DIM, STATE), jnp.float32)

    def forward(x_in, b_full, c_full, raw_rates):
        return run_blocks(x_in, b_full, c_full, raw_rates, bias_rates, resets, rate, d_skip, start_state)[0]
    _, pullback = jax.vjp(forward, activations, b_proj.astype(jnp.float32), c_proj.astype(jnp.float32), dt_raw)
    grad_input, grad_b, grad_c, grad_rate = pullback(cotangent)
    return (grad_input, grad_b, grad_c, grad_rate)
```

```python
from functools import partial

import jax
import jax.numpy as jnp
from jax import lax
from jax.experimental import pallas as pl
from jax.experimental.pallas import tpu as pltpu
from jax.sharding import PartitionSpec as P

BLOCK = 256
LOG2E = 1.4426950408889634
HI = lax.Precision.HIGHEST
F32 = jnp.float32
BF16 = jnp.bfloat16
NT = (((1,), (1,)), ((), ()))
VMEM_LIMIT = 50 * 1024 * 1024


def dot(a, b):
    return jnp.dot(a, b, preferred_element_type=F32)


def dot_nt(a, b):
    return lax.dot_general(a, b, NT, preferred_element_type=F32)


def dot_hi(a, b):
    return jnp.dot(a, b, precision=HI, preferred_element_type=F32)


def iota(shape, axis):
    return lax.broadcasted_iota(jnp.int32, shape, axis)


def summary_kernel(
    nb, x_ref, dy_ref, b_ref, c_ref, raw_ref, res_ref, ag_ref, bias_ref, alog_ref,
    rows_ref, aux_ref, added_ref, inject_ref, local_ref, back_ref, gam_ref, bt_s, ct_s,
):
    h = pl.program_id(0)
    heads = raw_ref.shape[0]

    @pl.when(h == 0)
    def _():
        upper = (iota((BLOCK, BLOCK), 0) <= iota((BLOCK, BLOCK), 1)).astype(F32)
        rate = jnp.exp(alog_ref[...])
        for b in range(nb):
            sl = slice(b * BLOCK, (b + 1) * BLOCK)
            bt_s[:, sl] = b_ref[sl, :].astype(F32).T
            ct_s[:, sl] = c_ref[sl, :].astype(F32).T
            onehot = (ag_ref[:, sl] == iota((bias_ref.shape[1], BLOCK), 0)).astype(F32)
            v = raw_ref[:, sl] + dot_hi(bias_ref[...], onehot)
            ev = jnp.exp(v)
            s = jnp.where(v > 15.0, v, jnp.log1p(ev))
            log_decay = -rate * s
            cum = dot_hi(log_decay, upper)
            res = jnp.broadcast_to(res_ref[:, sl].astype(F32), (8, BLOCK))
            ep = dot_hi(res, upper)[:1]
            cum2 = cum * LOG2E
            entry = jnp.where(ep < 0.5, jnp.exp(cum), 0.0)
            last = cum[:, BLOCK - 1 :]
            to_end = jnp.where(jnp.abs(ep - ep[:, BLOCK - 1 :]) < 0.5, jnp.exp(last - cum) * s, 0.0)
            rows_ref[:, b, :] = cum2
            rows_ref[:, nb + b, :] = cum2 - jnp.log2(s)
            rows_ref[:, 2 * nb + b, :] = entry
            rows_ref[:, 3 * nb + b, :] = to_end
            aux_ref[0, :, sl] = 1.0 / s
            aux_ref[1, :, sl] = ev / (1.0 + ev)
            aux_ref[2, :, sl] = jnp.broadcast_to(ep, (heads, BLOCK))

    added, inject, gammas = [], [], []
    for b in range(nb):
        sl = slice(b * BLOCK, (b + 1) * BLOCK)
        e_row = rows_ref[h, pl.ds(2 * nb + b, 1), :]
        t_row = rows_ref[h, pl.ds(3 * nb + b, 1), :]
        add = dot((bt_s[:, sl] * t_row).astype(BF16), x_ref[sl, :])
        inj = dot((ct_s[:, sl] * e_row).astype(BF16), dy_ref[sl, :]).astype(BF16)
        added_ref[0, b] = add
        inject_ref[0, b] = inj
        added.append(add)
        inject.append(inj.astype(F32))
        gammas.append(e_row[:, BLOCK - 1 :])
    local, back, total = added[0], inject[nb - 1], gammas[0]
    for b in range(1, nb):
        local = gammas[b] * local + added[b]
        total = total * gammas[b]
        back = gammas[nb - 1 - b] * back + inject[nb - 1 - b]
    local_ref[0] = local
    back_ref[0] = back
    gam_ref[0] = jnp.broadcast_to(total, gam_ref.shape[1:])


def grad_kernel(
    nb, x_ref, dy_ref, b_ref, c_ref, rows_ref, aux_ref, added_ref, inject_ref,
    entry_ref, exit_ref, alog_ref, dskip_ref,
    gx_ref, gb_ref, gc_ref, gr_ref,
    bt_s, ct_s, st_s, ds_s, dbt_s, dct_s, drow_s, dcol_s,
):
    h = pl.program_id(0)

    @pl.when(h == 0)
    def _():
        for b in range(nb):
            sl = slice(b * BLOCK, (b + 1) * BLOCK)
            bt_s[:, sl] = b_ref[sl, :].astype(F32).T
            ct_s[:, sl] = c_ref[sl, :].astype(F32).T
            ep = aux_ref[2, :8, sl]
            ep_col = ep.T[:, :1]
            mask = (iota((BLOCK, BLOCK), 0) <= iota((BLOCK, BLOCK), 1)) & (
                jnp.abs(ep_col - ep[:1]) < 0.5
            )
            st_s[b] = jnp.where(mask, dot_nt(b_ref[sl, :], c_ref[sl, :]), 0.0)
        ds_s[...] = jnp.zeros_like(ds_s)
        dbt_s[...] = jnp.zeros_like(dbt_s)
        dct_s[...] = jnp.zeros_like(dct_s)

    rows = rows_ref[0]
    cols = rows.T
    ones = jnp.ones((8, x_ref.shape[1]), BF16)
    d_h = dskip_ref[h]
    gam = [rows[2 * nb + b : 2 * nb + b + 1, BLOCK - 1 :] for b in range(nb)]
    states = [entry_ref[0]]
    for b in range(nb):
        states.append(gam[b] * states[b] + added_ref[0, b])
    grads = [exit_ref[0]]
    for b in range(nb - 1, 0, -1):
        grads.insert(0, gam[b] * grads[0] + inject_ref[0, b].astype(F32))
    for b in range(nb):
        sl = slice(b * BLOCK, (b + 1) * BLOCK)
        x, dy = x_ref[sl, :], dy_ref[sl, :]
        g16 = grads[b].astype(BF16)
        s16 = states[b].astype(BF16)
        dmt = dot_nt(x, dy)
        decay = jnp.exp2(rows[b : b + 1] - cols[:, nb + b : nb + b + 1])
        mt = st_s[b] * decay
        ds_s[b] += dmt * decay
        row = jnp.sum(dmt * mt, axis=0, keepdims=True)
        dcs = dot_nt(s16, dy) * rows[2 * nb + b : 2 * nb + b + 1]
        dct_s[:, sl] += dcs
        row += jnp.sum(dcs * ct_s[:, sl], axis=0, keepdims=True)
        row_end = jnp.sum(jnp.sum(grads[b] * states[b + 1], axis=0, keepdims=True), axis=1, keepdims=True)
        dbt_s[:, sl] += dot_nt(g16, x) * rows[3 * nb + b : 3 * nb + b + 1]
        dx = dot(mt.astype(BF16), dy) + cols[:, 3 * nb + b : 3 * nb + b + 1] * dot(b_ref[sl, :], g16)
        z = x.astype(F32) * dx
        zh = z.astype(BF16)
        zl = (z - zh.astype(F32)).astype(BF16)
        col = (dot_nt(ones, zh) + dot_nt(ones, zl))[:1]
        gx_ref[sl, :] = (dx + d_h * dy.astype(F32)).astype(BF16)
        last = iota((1, BLOCK), 1) == BLOCK - 1
        drow_s[pl.ds(h, 1), sl] = row - col + jnp.where(last, row_end, 0.0)
        dcol_s[pl.ds(h, 1), sl] = col

    @pl.when(h == pl.num_programs(0) - 1)
    def _():
        lower = (iota((BLOCK, BLOCK), 0) >= iota((BLOCK, BLOCK), 1)).astype(F32)
        rate = jnp.exp(alog_ref[...])
        for b in range(nb):
            sl = slice(b * BLOCK, (b + 1) * BLOCK)
            dlog = dot_hi(drow_s[:, sl], lower)
            gr_ref[:, sl] = (dcol_s[:, sl] * aux_ref[0, :, sl] - rate * dlog) * aux_ref[1, :, sl]
            ep = aux_ref[2, :8, sl]
            ep_col = ep.T[:, :1]
            mask = (iota((BLOCK, BLOCK), 0) <= iota((BLOCK, BLOCK), 1)) & (
                jnp.abs(ep_col - ep[:1]) < 0.5
            )
            ds = jnp.where(mask, ds_s[b], 0.0)
            dh = ds.astype(BF16)
            dl = (ds - dh.astype(F32)).astype(BF16)
            ct = ct_s[:, sl].astype(BF16)
            bt = bt_s[:, sl].astype(BF16)
            gb_ref[sl, :] = (dbt_s[:, sl] + dot_nt(ct, dh) + dot_nt(ct, dl)).T
            gc_ref[sl, :] = (dct_s[:, sl] + dot(bt, dh) + dot(bt, dl)).T


def whole(shape):
    return pl.BlockSpec(shape, lambda h: (0,) * len(shape))


def per_head(shape):
    return pl.BlockSpec((1,) + shape, lambda h: (h,) + (0,) * len(shape))


def entering(value, axis, backward):
    count, mine = (lax.axis_size(axis), lax.axis_index(axis))
    decay, state = jax.tree.map(lambda part: lax.all_gather(part, axis), value)
    if backward:
        decay, state = decay[::-1], state[::-1]
        mine = count - 1 - mine
    total = jnp.zeros_like(value[1])
    for k in range(count - 1):
        longer = decay[k][:, :1] * total + state[k]
        total = jnp.where(k < mine, longer, total)
    return total


def on_device(
    activations, cotangent, b_proj, c_proj, dt_raw, resets, agents, agent_bias, a_log, d_skip
):
    heads = dt_raw.shape[0]
    width = activations.shape[1] // heads
    n = b_proj.shape[1]
    tokens = activations.shape[0]
    nb = tokens // BLOCK
    xspec = pl.BlockSpec((tokens, width), lambda h: (0, h))
    alog = a_log[:, None]
    sds = jax.ShapeDtypeStruct
    rows, aux, added, inject, local, back, gam = pl.pallas_call(
        partial(summary_kernel, nb),
        grid=(heads,),
        in_specs=[
            xspec, xspec, whole((tokens, n)), whole((tokens, n)), whole((heads, tokens)),
            whole((1, tokens)), whole((1, tokens)), whole(agent_bias.shape), whole((heads, 1)),
        ],
        out_specs=[
            whole((heads, 4 * nb, BLOCK)), whole((3, heads, tokens)), per_head((nb, n, width)),
            per_head((nb, n, width)), per_head((n, width)), per_head((n, width)), per_head((8, width)),
        ],
        out_shape=[
            sds((heads, 4 * nb, BLOCK), F32), sds((3, heads, tokens), F32),
            sds((heads, nb, n, width), F32), sds((heads, nb, n, width), BF16),
            sds((heads, n, width), F32), sds((heads, n, width), F32), sds((heads, 8, width), F32),
        ],
        scratch_shapes=[pltpu.VMEM((n, tokens), F32), pltpu.VMEM((n, tokens), F32)],
        compiler_params=pltpu.CompilerParams(vmem_limit_bytes=VMEM_LIMIT),
    )(
        activations, cotangent, b_proj, c_proj, dt_raw, resets[None], agents[None], agent_bias, alog
    )
    entry = entering((gam, local), ("seq", "rep"), False)
    exit_grad = entering((gam, back), ("seq", "rep"), True)
    grad_x, grad_b, grad_c, grad_rate = pl.pallas_call(
        partial(grad_kernel, nb),
        grid=(heads,),
        in_specs=[
            xspec, xspec, whole((tokens, n)), whole((tokens, n)), per_head((4 * nb, BLOCK)),
            whole((3, heads, tokens)), per_head((nb, n, width)), per_head((nb, n, width)),
            per_head((n, width)), per_head((n, width)), whole((heads, 1)),
            pl.BlockSpec(memory_space=pltpu.SMEM),
        ],
        out_specs=[xspec, whole((tokens, n)), whole((tokens, n)), whole((heads, tokens))],
        out_shape=[
            sds(activations.shape, BF16), sds((tokens, n), F32), sds((tokens, n), F32),
            sds((heads, tokens), F32),
        ],
        scratch_shapes=[
            pltpu.VMEM((n, tokens), F32), pltpu.VMEM((n, tokens), F32),
            pltpu.VMEM((nb, BLOCK, BLOCK), F32), pltpu.VMEM((nb, BLOCK, BLOCK), F32),
            pltpu.VMEM((n, tokens), F32), pltpu.VMEM((n, tokens), F32),
            pltpu.VMEM((heads, tokens), F32), pltpu.VMEM((heads, tokens), F32),
        ],
        compiler_params=pltpu.CompilerParams(vmem_limit_bytes=VMEM_LIMIT),
    )(
        activations, cotangent, b_proj, c_proj, rows, aux, added, inject, entry, exit_grad, alog,
        d_skip,
    )
    grad_b, grad_c = lax.psum((grad_b, grad_c), "head")
    return (grad_x, grad_b, grad_c, grad_rate)


def solution(mesh):
    tok = ("grp", "seq", "rep")
    return jax.shard_map(
        on_device,
        mesh=mesh,
        in_specs=(
            P(tok, "head"), P(tok, "head"), P(tok, None), P(tok, None), P("head", tok),
            P(tok), P(tok), P("head", None), P("head"), P("head"),
        ),
        out_specs=(P(tok, "head"), P(tok, None), P(tok, None), P("head", tok)),
        check_vma=False,
    )
```

```python
from functools import partial

import jax
import jax.numpy as jnp
from jax import lax
from jax.experimental import pallas as pl
from jax.experimental.pallas import tpu as pltpu
from jax.sharding import PartitionSpec as P

BLOCK = 256
LOG2E = 1.4426950408889634
HI = lax.Precision.HIGHEST
F32 = jnp.float32
BF16 = jnp.bfloat16
NT = (((1,), (1,)), ((), ()))
VMEM_LIMIT = 50 * 1024 * 1024


def dot(a, b):
    return jnp.dot(a, b, preferred_element_type=F32)


def dot_nt(a, b):
    return lax.dot_general(a, b, NT, preferred_element_type=F32)


def dot_hi(a, b):
    return jnp.dot(a, b, precision=HI, preferred_element_type=F32)


def iota(shape, axis):
    return lax.broadcasted_iota(jnp.int32, shape, axis)


def summary_kernel(
    nb, x_ref, dy_ref, b_ref, c_ref, raw_ref, res_ref, ag_ref, bias_ref, alog_ref,
    rows_ref, aux_ref, added_ref, inject_ref, local_ref, back_ref, gam_ref, bt_s, ct_s,
):
    h = pl.program_id(0)
    heads = raw_ref.shape[0]

    @pl.when(h == 0)
    def _():
        upper = (iota((BLOCK, BLOCK), 0) <= iota((BLOCK, BLOCK), 1)).astype(F32)
        rate = jnp.exp(alog_ref[...])
        for b in range(nb):
            sl = slice(b * BLOCK, (b + 1) * BLOCK)
            bt_s[:, sl] = b_ref[sl, :].astype(F32).T
            ct_s[:, sl] = c_ref[sl, :].astype(F32).T
            onehot = (ag_ref[:, sl] == iota((bias_ref.shape[1], BLOCK), 0)).astype(F32)
            v = raw_ref[:, sl] + dot_hi(bias_ref[...], onehot)
            ev = jnp.exp(v)
            s = jnp.where(v > 15.0, v, jnp.log1p(ev))
            log_decay = -rate * s
            cum = dot_hi(log_decay, upper)
            res = jnp.broadcast_to(res_ref[:, sl].astype(F32), (8, BLOCK))
            ep = dot_hi(res, upper)[:1]
            cum2 = cum * LOG2E
            entry = jnp.where(ep < 0.5, jnp.exp(cum), 0.0)
            last = cum[:, BLOCK - 1 :]
            to_end = jnp.where(jnp.abs(ep - ep[:, BLOCK - 1 :]) < 0.5, jnp.exp(last - cum) * s, 0.0)
            rows_ref[:, b, :] = cum2
            rows_ref[:, nb + b, :] = cum2 - jnp.log2(s)
            rows_ref[:, 2 * nb + b, :] = entry
            rows_ref[:, 3 * nb + b, :] = to_end
            aux_ref[0, :, sl] = 1.0 / s
            aux_ref[1, :, sl] = ev / (1.0 + ev)
            aux_ref[2, :, sl] = jnp.broadcast_to(ep, (heads, BLOCK))

    added, inject, gammas = [], [], []
    for b in range(nb):
        sl = slice(b * BLOCK, (b + 1) * BLOCK)
        e_row = rows_ref[h, pl.ds(2 * nb + b, 1), :]
        t_row = rows_ref[h, pl.ds(3 * nb + b, 1), :]
        add = dot((bt_s[:, sl] * t_row).astype(BF16), x_ref[sl, :])
        inj = dot((ct_s[:, sl] * e_row).astype(BF16), dy_ref[sl, :]).astype(BF16)
        added_ref[0, b] = add
        inject_ref[0, b] = inj
        added.append(add)
        inject.append(inj.astype(F32))
        gammas.append(e_row[:, BLOCK - 1 :])
    local, back, total = added[0], inject[nb - 1], gammas[0]
    for b in range(1, nb):
        local = gammas[b] * local + added[b]
        total = total * gammas[b]
        back = gammas[nb - 1 - b] * back + inject[nb - 1 - b]
    local_ref[0] = local
    back_ref[0] = back
    gam_ref[0] = jnp.broadcast_to(total, gam_ref.shape[1:])


def grad_kernel(
    nb, x_ref, dy_ref, b_ref, c_ref, rows_ref, aux_ref, added_ref, inject_ref,
    entry_ref, exit_ref, alog_ref, dskip_ref,
    gx_ref, gb_ref, gc_ref, gr_ref,
    bt_s, ct_s, st_s, ds_s, dbt_s, dct_s, drow_s, dcol_s,
):
    h = pl.program_id(0)

    @pl.when(h == 0)
    def _():
        for b in range(nb):
            sl = slice(b * BLOCK, (b + 1) * BLOCK)
            bt_s[:, sl] = b_ref[sl, :].astype(F32).T
            ct_s[:, sl] = c_ref[sl, :].astype(F32).T
            ep = aux_ref[2, :8, sl]
            ep_col = ep.T[:, :1]
            mask = (iota((BLOCK, BLOCK), 0) <= iota((BLOCK, BLOCK), 1)) & (
                jnp.abs(ep_col - ep[:1]) < 0.5
            )
            st_s[b] = jnp.where(mask, dot_nt(b_ref[sl, :], c_ref[sl, :]), 0.0)
        ds_s[...] = jnp.zeros_like(ds_s)
        dbt_s[...] = jnp.zeros_like(dbt_s)
        dct_s[...] = jnp.zeros_like(dct_s)

    rows = rows_ref[0]
    cols = rows.T
    ones = jnp.ones((8, x_ref.shape[1]), BF16)
    d_h = dskip_ref[h]
    gam = [rows[2 * nb + b : 2 * nb + b + 1, BLOCK - 1 :] for b in range(nb)]
    states = [entry_ref[0]]
    for b in range(nb):
        states.append(gam[b] * states[b] + added_ref[0, b])
    grads = [exit_ref[0]]
    for b in range(nb - 1, 0, -1):
        grads.insert(0, gam[b] * grads[0] + inject_ref[0, b].astype(F32))
    for b in range(nb):
        sl = slice(b * BLOCK, (b + 1) * BLOCK)
        x, dy = x_ref[sl, :], dy_ref[sl, :]
        g16 = grads[b].astype(BF16)
        s16 = states[b].astype(BF16)
        dmt = dot_nt(x, dy)
        decay = jnp.exp2(rows[b : b + 1] - cols[:, nb + b : nb + b + 1])
        mt = st_s[b] * decay
        ds_s[b] += dmt * decay
        row = jnp.sum(dmt * mt, axis=0, keepdims=True)
        dcs = dot_nt(s16, dy) * rows[2 * nb + b : 2 * nb + b + 1]
        dct_s[:, sl] += dcs
        row += jnp.sum(dcs * ct_s[:, sl], axis=0, keepdims=True)
        row_end = jnp.sum(jnp.sum(grads[b] * states[b + 1], axis=0, keepdims=True), axis=1, keepdims=True)
        dbt_s[:, sl] += dot_nt(g16, x) * rows[3 * nb + b : 3 * nb + b + 1]
        dx = dot(mt.astype(BF16), dy) + cols[:, 3 * nb + b : 3 * nb + b + 1] * dot(b_ref[sl, :], g16)
        z = x.astype(F32) * dx
        zh = z.astype(BF16)
        zl = (z - zh.astype(F32)).astype(BF16)
        col = (dot_nt(ones, zh) + dot_nt(ones, zl))[:1]
        gx_ref[sl, :] = (dx + d_h * dy.astype(F32)).astype(BF16)
        last = iota((1, BLOCK), 1) == BLOCK - 1
        drow_s[pl.ds(h, 1), sl] = row - col + jnp.where(last, row_end, 0.0)
        dcol_s[pl.ds(h, 1), sl] = col

    @pl.when(h == pl.num_programs(0) - 1)
    def _():
        lower = (iota((BLOCK, BLOCK), 0) >= iota((BLOCK, BLOCK), 1)).astype(F32)
        rate = jnp.exp(alog_ref[...])
        for b in range(nb):
            sl = slice(b * BLOCK, (b + 1) * BLOCK)
            dlog = dot_hi(drow_s[:, sl], lower)
            gr_ref[:, sl] = (dcol_s[:, sl] * aux_ref[0, :, sl] - rate * dlog) * aux_ref[1, :, sl]
            ep = aux_ref[2, :8, sl]
            ep_col = ep.T[:, :1]
            mask = (iota((BLOCK, BLOCK), 0) <= iota((BLOCK, BLOCK), 1)) & (
                jnp.abs(ep_col - ep[:1]) < 0.5
            )
            ds = jnp.where(mask, ds_s[b], 0.0)
            dh = ds.astype(BF16)
            dl = (ds - dh.astype(F32)).astype(BF16)
            ct = ct_s[:, sl].astype(BF16)
            bt = bt_s[:, sl].astype(BF16)
            gb_ref[sl, :] = (dbt_s[:, sl] + dot_nt(ct, dh) + dot_nt(ct, dl)).T
            gc_ref[sl, :] = (dct_s[:, sl] + dot(bt, dh) + dot(bt, dl)).T


def whole(shape):
    return pl.BlockSpec(shape, lambda h: (0,) * len(shape))


def per_head(shape):
    return pl.BlockSpec((1,) + shape, lambda h: (h,) + (0,) * len(shape))


MESH = pl.DeviceIdType.MESH
AHEAD = 2


def chain_kernel(
    gam_ref, local_ref, back_ref, entry_ref, exit_ref,
    fin_s, fout_s, bin_s, bout_s, fsend, frecv, bsend, brecv,
):
    reps = lax.axis_size("rep")
    last = lax.axis_size("seq") * reps - 1
    mine = lax.axis_index("seq") * reps + lax.axis_index("rep")
    steps = fsend.shape[0]
    per = gam_ref.shape[0] // steps

    def place(index):
        return {"seq": index // reps, "rep": index % reps}

    barrier = pltpu.get_barrier_semaphore()

    @pl.when(mine > 0)
    def _():
        pl.semaphore_signal(barrier, inc=1, device_id=place(mine - 1), device_id_type=MESH)

    @pl.when(mine < last)
    def _():
        pl.semaphore_signal(barrier, inc=1, device_id=place(mine + 1), device_id_type=MESH)

    edge = (mine == 0) | (mine == last)

    @pl.when(edge)
    def _():
        pl.semaphore_wait(barrier, 1)

    @pl.when(jnp.logical_not(edge))
    def _():
        pl.semaphore_wait(barrier, 2)

    def hop(k, out_s, in_s, send, recv, target):
        sl = pl.ds(k * per, per)
        return pltpu.make_async_remote_copy(
            src_ref=out_s.at[sl], dst_ref=in_s.at[sl], send_sem=send.at[k], recv_sem=recv.at[k],
            device_id=place(target), device_id_type=MESH,
        )

    def advance(k, first, final, target, own_ref, got_ref, out_s, in_s, send, recv):
        sl = pl.ds(k * per, per)

        @pl.when(first)
        def _():
            got_ref[sl] = jnp.zeros_like(got_ref[sl])
            out_s[sl] = own_ref[sl]

        @pl.when(jnp.logical_not(first))
        def _():
            hop(k, out_s, in_s, send, recv, target).wait_recv()
            got = in_s[sl]
            got_ref[sl] = got
            out_s[sl] = gam_ref[sl, :1, :] * got + own_ref[sl]

        @pl.when(jnp.logical_not(final))
        def _():
            hop(k, out_s, in_s, send, recv, target).start()

    right = jnp.minimum(mine + 1, last)
    left = jnp.maximum(mine - 1, 0)

    def tick(t, _):
        kf = t - mine * AHEAD
        kb = t - (last - mine) * AHEAD

        @pl.when((kf >= 0) & (kf < steps))
        def _():
            advance(kf, mine == 0, mine == last, right, local_ref, entry_ref, fout_s, fin_s, fsend, frecv)

        @pl.when((kb >= 0) & (kb < steps))
        def _():
            advance(kb, mine == last, mine == 0, left, back_ref, exit_ref, bout_s, bin_s, bsend, brecv)

        return 0

    lax.fori_loop(0, last * AHEAD + steps, tick, 0)

    def drain(k, _):
        @pl.when(mine < last)
        def _():
            hop(k, fout_s, fin_s, fsend, frecv, right).wait_send()

        @pl.when(mine > 0)
        def _():
            hop(k, bout_s, bin_s, bsend, brecv, left).wait_send()

        return 0

    lax.fori_loop(0, steps, drain, 0)


def chain(gam, local, back):
    heads = gam.shape[0]
    steps = min(8, heads)
    spec = pl.BlockSpec(memory_space=pltpu.VMEM)
    out = jax.ShapeDtypeStruct(local.shape, F32)
    return pl.pallas_call(
        chain_kernel,
        in_specs=[spec] * 3,
        out_specs=[spec] * 2,
        out_shape=[out, out],
        scratch_shapes=[pltpu.VMEM(local.shape, F32)] * 4 + [pltpu.SemaphoreType.DMA((steps,))] * 4,
        compiler_params=pltpu.CompilerParams(
            collective_id=0, has_side_effects=True, vmem_limit_bytes=VMEM_LIMIT
        ),
    )(gam, local, back)


def pair_kernel(gb_ref, gc_ref, ob_ref, oc_ref, got_b, got_c, send, recv):
    other = {"head": 1 - lax.axis_index("head")}
    barrier = pltpu.get_barrier_semaphore()
    pl.semaphore_signal(barrier, inc=1, device_id=other, device_id_type=MESH)
    pl.semaphore_wait(barrier, 1)
    pieces = send.shape[1]
    rows = gb_ref.shape[0] // pieces
    trio = ((gb_ref, got_b, ob_ref), (gc_ref, got_c, oc_ref))

    def hop(i, k):
        sl = slice(k * rows, (k + 1) * rows)
        return pltpu.make_async_remote_copy(
            src_ref=trio[i][0].at[sl], dst_ref=trio[i][1].at[sl], send_sem=send.at[i, k],
            recv_sem=recv.at[i, k], device_id=other, device_id_type=MESH,
        )

    copies = [(i, k, hop(i, k)) for i in range(2) for k in range(pieces)]
    for _, _, copy in copies:
        copy.start()
    for i, k, copy in copies:
        sl = slice(k * rows, (k + 1) * rows)
        copy.wait_recv()
        trio[i][2][sl] = trio[i][0][sl] + trio[i][1][sl]
    for _, _, copy in copies:
        copy.wait_send()


def over_heads(grad_b, grad_c):
    if lax.axis_size("head") != 2:
        return lax.psum((grad_b, grad_c), "head")
    spec = pl.BlockSpec(memory_space=pltpu.VMEM)
    out = jax.ShapeDtypeStruct(grad_b.shape, F32)
    return pl.pallas_call(
        pair_kernel,
        in_specs=[spec] * 2,
        out_specs=[spec] * 2,
        out_shape=[out, out],
        scratch_shapes=[pltpu.VMEM(grad_b.shape, F32)] * 2 + [pltpu.SemaphoreType.DMA((2, 4))] * 2,
        compiler_params=pltpu.CompilerParams(
            collective_id=1, has_side_effects=True, vmem_limit_bytes=VMEM_LIMIT
        ),
    )(grad_b, grad_c)


def on_device(
    activations, cotangent, b_proj, c_proj, dt_raw, resets, agents, agent_bias, a_log, d_skip
):
    heads = dt_raw.shape[0]
    width = activations.shape[1] // heads
    n = b_proj.shape[1]
    tokens = activations.shape[0]
    nb = tokens // BLOCK
    xspec = pl.BlockSpec((tokens, width), lambda h: (0, h))
    alog = a_log[:, None]
    sds = jax.ShapeDtypeStruct
    rows, aux, added, inject, local, back, gam = pl.pallas_call(
        partial(summary_kernel, nb),
        grid=(heads,),
        in_specs=[
            xspec, xspec, whole((tokens, n)), whole((tokens, n)), whole((heads, tokens)),
            whole((1, tokens)), whole((1, tokens)), whole(agent_bias.shape), whole((heads, 1)),
        ],
        out_specs=[
            whole((heads, 4 * nb, BLOCK)), whole((3, heads, tokens)), per_head((nb, n, width)),
            per_head((nb, n, width)), per_head((n, width)), per_head((n, width)), per_head((8, width)),
        ],
        out_shape=[
            sds((heads, 4 * nb, BLOCK), F32), sds((3, heads, tokens), F32),
            sds((heads, nb, n, width), F32), sds((heads, nb, n, width), BF16),
            sds((heads, n, width), F32), sds((heads, n, width), F32), sds((heads, 8, width), F32),
        ],
        scratch_shapes=[pltpu.VMEM((n, tokens), F32), pltpu.VMEM((n, tokens), F32)],
        compiler_params=pltpu.CompilerParams(vmem_limit_bytes=VMEM_LIMIT),
    )(
        activations, cotangent, b_proj, c_proj, dt_raw, resets[None], agents[None], agent_bias, alog
    )
    entry, exit_grad = chain(gam, local, back)
    grad_x, grad_b, grad_c, grad_rate = pl.pallas_call(
        partial(grad_kernel, nb),
        grid=(heads,),
        in_specs=[
            xspec, xspec, whole((tokens, n)), whole((tokens, n)), per_head((4 * nb, BLOCK)),
            whole((3, heads, tokens)), per_head((nb, n, width)), per_head((nb, n, width)),
            per_head((n, width)), per_head((n, width)), whole((heads, 1)),
            pl.BlockSpec(memory_space=pltpu.SMEM),
        ],
        out_specs=[xspec, whole((tokens, n)), whole((tokens, n)), whole((heads, tokens))],
        out_shape=[
            sds(activations.shape, BF16), sds((tokens, n), F32), sds((tokens, n), F32),
            sds((heads, tokens), F32),
        ],
        scratch_shapes=[
            pltpu.VMEM((n, tokens), F32), pltpu.VMEM((n, tokens), F32),
            pltpu.VMEM((nb, BLOCK, BLOCK), F32), pltpu.VMEM((nb, BLOCK, BLOCK), F32),
            pltpu.VMEM((n, tokens), F32), pltpu.VMEM((n, tokens), F32),
            pltpu.VMEM((heads, tokens), F32), pltpu.VMEM((heads, tokens), F32),
        ],
        compiler_params=pltpu.CompilerParams(vmem_limit_bytes=VMEM_LIMIT),
    )(
        activations, cotangent, b_proj, c_proj, rows, aux, added, inject, entry, exit_grad, alog,
        d_skip,
    )
    grad_b, grad_c = over_heads(grad_b, grad_c)
    return (grad_x, grad_b, grad_c, grad_rate)


def solution(mesh):
    tok = ("grp", "seq", "rep")
    return jax.shard_map(
        on_device,
        mesh=mesh,
        in_specs=(
            P(tok, "head"), P(tok, "head"), P(tok, None), P(tok, None), P("head", tok),
            P(tok), P(tok), P("head", None), P("head"), P("head"),
        ),
        out_specs=(P(tok, "head"), P(tok, None), P(tok, None), P("head", tok)),
        check_vma=False,
    )
```

```python
from functools import partial

import jax
import jax.numpy as jnp
from jax import lax
from jax.experimental import pallas as pl
from jax.experimental.pallas import tpu as pltpu
from jax.sharding import PartitionSpec as P

BLOCK = 256
LOG2E = 1.4426950408889634
HI = lax.Precision.HIGHEST
F32 = jnp.float32
BF16 = jnp.bfloat16
NT = (((1,), (1,)), ((), ()))
VMEM_LIMIT = 62 * 1024 * 1024


def dot(a, b):
    return jnp.dot(a, b, preferred_element_type=F32)


def dot_nt(a, b):
    return lax.dot_general(a, b, NT, preferred_element_type=F32)


def dot_hi(a, b):
    return jnp.dot(a, b, precision=HI, preferred_element_type=F32)


def iota(shape, axis):
    return lax.broadcasted_iota(jnp.int32, shape, axis)


def summary_kernel(
    nb, x_ref, dy_ref, b_ref, c_ref, raw_ref, res_ref, ag_ref, bias_ref, alog_ref,
    rows_ref, aux_ref, added_ref, inject_ref, local_ref, back_ref, gam_ref, bt_s, ct_s,
):
    h = pl.program_id(0)
    heads = raw_ref.shape[0]

    @pl.when(h == 0)
    def _():
        upper = (iota((BLOCK, BLOCK), 0) <= iota((BLOCK, BLOCK), 1)).astype(F32)
        rate = jnp.exp(alog_ref[...])
        for b in range(nb):
            sl = slice(b * BLOCK, (b + 1) * BLOCK)
            bt_s[:, sl] = b_ref[sl, :].astype(F32).T
            ct_s[:, sl] = c_ref[sl, :].astype(F32).T
            onehot = (ag_ref[:, sl] == iota((bias_ref.shape[1], BLOCK), 0)).astype(F32)
            v = raw_ref[:, sl] + dot_hi(bias_ref[...], onehot)
            ev = jnp.exp(v)
            s = jnp.where(v > 15.0, v, jnp.log1p(ev))
            log_decay = -rate * s
            cum = dot_hi(log_decay, upper)
            res = jnp.broadcast_to(res_ref[:, sl].astype(F32), (8, BLOCK))
            ep = dot_hi(res, upper)[:1]
            cum2 = cum * LOG2E
            entry = jnp.where(ep < 0.5, jnp.exp(cum), 0.0)
            last = cum[:, BLOCK - 1 :]
            to_end = jnp.where(jnp.abs(ep - ep[:, BLOCK - 1 :]) < 0.5, jnp.exp(last - cum) * s, 0.0)
            rows_ref[:, b, :] = cum2
            rows_ref[:, nb + b, :] = cum2 - jnp.log2(s)
            rows_ref[:, 2 * nb + b, :] = entry
            rows_ref[:, 3 * nb + b, :] = to_end
            aux_ref[0, :, sl] = 1.0 / s
            aux_ref[1, :, sl] = ev / (1.0 + ev)
            aux_ref[2, :, sl] = jnp.broadcast_to(ep, (heads, BLOCK))

    added, inject, gammas = [], [], []
    for b in range(nb):
        sl = slice(b * BLOCK, (b + 1) * BLOCK)
        e_row = rows_ref[h, pl.ds(2 * nb + b, 1), :]
        t_row = rows_ref[h, pl.ds(3 * nb + b, 1), :]
        add = dot((bt_s[:, sl] * t_row).astype(BF16), x_ref[sl, :])
        inj = dot((ct_s[:, sl] * e_row).astype(BF16), dy_ref[sl, :]).astype(BF16)
        added_ref[0, b] = add
        inject_ref[0, b] = inj
        added.append(add)
        inject.append(inj.astype(F32))
        gammas.append(e_row[:, BLOCK - 1 :])
    local, back, total = added[0], inject[nb - 1], gammas[0]
    for b in range(1, nb):
        local = gammas[b] * local + added[b]
        total = total * gammas[b]
        back = gammas[nb - 1 - b] * back + inject[nb - 1 - b]
    local_ref[0] = local
    back_ref[0] = back
    gam_ref[0] = jnp.broadcast_to(total, gam_ref.shape[1:])


def grad_kernel(
    nb, x_ref, dy_ref, b_ref, c_ref, rows_ref, aux_ref, added_ref, inject_ref,
    entry_ref, exit_ref, alog_ref, dskip_ref, dxi_ref, ds_ref, row_ref,
    gx_ref, gb_ref, gc_ref, gr_ref,
    bt_s, ct_s, dbt_s, dct_s, drow_s, dcol_s,
):
    h = pl.program_id(0)

    @pl.when(h == 0)
    def _():
        for b in range(nb):
            sl = slice(b * BLOCK, (b + 1) * BLOCK)
            bt_s[:, sl] = b_ref[sl, :].astype(F32).T
            ct_s[:, sl] = c_ref[sl, :].astype(F32).T
        dbt_s[...] = jnp.zeros_like(dbt_s)
        dct_s[...] = jnp.zeros_like(dct_s)

    rows = rows_ref[0]
    cols = rows.T
    ones = jnp.ones((8, x_ref.shape[1]), BF16)
    d_h = dskip_ref[h]
    gam = [rows[2 * nb + b : 2 * nb + b + 1, BLOCK - 1 :] for b in range(nb)]
    states = [entry_ref[0]]
    for b in range(nb):
        states.append(gam[b] * states[b] + added_ref[0, b])
    grads = [exit_ref[0]]
    for b in range(nb - 1, 0, -1):
        grads.insert(0, gam[b] * grads[0] + inject_ref[0, b].astype(F32))
    for b in range(nb):
        sl = slice(b * BLOCK, (b + 1) * BLOCK)
        x, dy = x_ref[sl, :], dy_ref[sl, :]
        g16 = grads[b].astype(BF16)
        s16 = states[b].astype(BF16)
        dcs = dot_nt(s16, dy) * rows[2 * nb + b : 2 * nb + b + 1]
        dct_s[:, sl] += dcs
        row = row_ref[pl.ds(h, 1), sl] + jnp.sum(dcs * ct_s[:, sl], axis=0, keepdims=True)
        row_end = jnp.sum(jnp.sum(grads[b] * states[b + 1], axis=0, keepdims=True), axis=1, keepdims=True)
        dbt_s[:, sl] += dot_nt(g16, x) * rows[3 * nb + b : 3 * nb + b + 1]
        dx = dxi_ref[sl, :].astype(F32) + cols[:, 3 * nb + b : 3 * nb + b + 1] * dot(b_ref[sl, :], g16)
        z = x.astype(F32) * dx
        zh = z.astype(BF16)
        zl = (z - zh.astype(F32)).astype(BF16)
        col = (dot_nt(ones, zh) + dot_nt(ones, zl))[:1]
        gx_ref[sl, :] = (dx + d_h * dy.astype(F32)).astype(BF16)
        last = iota((1, BLOCK), 1) == BLOCK - 1
        drow_s[pl.ds(h, 1), sl] = row - col + jnp.where(last, row_end, 0.0)
        dcol_s[pl.ds(h, 1), sl] = col

    @pl.when(h == pl.num_programs(0) - 1)
    def _():
        lower = (iota((BLOCK, BLOCK), 0) >= iota((BLOCK, BLOCK), 1)).astype(F32)
        rate = jnp.exp(alog_ref[...])
        for b in range(nb):
            sl = slice(b * BLOCK, (b + 1) * BLOCK)
            dlog = dot_hi(drow_s[:, sl], lower)
            gr_ref[:, sl] = (dcol_s[:, sl] * aux_ref[0, :, sl] - rate * dlog) * aux_ref[1, :, sl]
            ep = aux_ref[2, :8, sl]
            ep_col = ep.T[:, :1]
            mask = (iota((BLOCK, BLOCK), 0) <= iota((BLOCK, BLOCK), 1)) & (
                jnp.abs(ep_col - ep[:1]) < 0.5
            )
            ds = jnp.where(mask, ds_ref[b], 0.0)
            dh = ds.astype(BF16)
            dl = (ds - dh.astype(F32)).astype(BF16)
            ct = ct_s[:, sl].astype(BF16)
            bt = bt_s[:, sl].astype(BF16)
            gb_ref[sl, :] = (dbt_s[:, sl] + dot_nt(ct, dh) + dot_nt(ct, dl)).T
            gc_ref[sl, :] = (dct_s[:, sl] + dot(bt, dh) + dot(bt, dl)).T


def whole(shape):
    return pl.BlockSpec(shape, lambda h: (0,) * len(shape))


def per_head(shape):
    return pl.BlockSpec((1,) + shape, lambda h: (h,) + (0,) * len(shape))


MESH = pl.DeviceIdType.MESH
AHEAD = 2


def chain_kernel(
    gam_ref, local_ref, back_ref, x_ref, dy_ref, b_ref, c_ref, rows_ref, aux_ref,
    entry_ref, exit_ref, dxi_ref, ds_ref, row_ref, st_s,
    fin_s, fout_s, bin_s, bout_s, fsend, frecv, bsend, brecv,
):
    reps = lax.axis_size("rep")
    last = lax.axis_size("seq") * reps - 1
    mine = lax.axis_index("seq") * reps + lax.axis_index("rep")
    steps = fsend.shape[0]
    heads, _, width = gam_ref.shape
    per = heads // steps
    nb = ds_ref.shape[0]

    def place(index):
        return {"seq": index // reps, "rep": index % reps}

    barrier = pltpu.get_barrier_semaphore()

    @pl.when(mine > 0)
    def _():
        pl.semaphore_signal(barrier, inc=1, device_id=place(mine - 1), device_id_type=MESH)

    @pl.when(mine < last)
    def _():
        pl.semaphore_signal(barrier, inc=1, device_id=place(mine + 1), device_id_type=MESH)

    edge = (mine == 0) | (mine == last)

    @pl.when(edge)
    def _():
        pl.semaphore_wait(barrier, 1)

    @pl.when(jnp.logical_not(edge))
    def _():
        pl.semaphore_wait(barrier, 2)

    def hop(k, out_s, in_s, send, recv, target):
        sl = pl.ds(k * per, per)
        return pltpu.make_async_remote_copy(
            src_ref=out_s.at[sl], dst_ref=in_s.at[sl], send_sem=send.at[k], recv_sem=recv.at[k],
            device_id=place(target), device_id_type=MESH,
        )

    def advance(k, first, final, target, own_ref, got_ref, out_s, in_s, send, recv):
        sl = pl.ds(k * per, per)

        @pl.when(first)
        def _():
            got_ref[sl] = jnp.zeros_like(got_ref[sl])
            out_s[sl] = own_ref[sl]

        @pl.when(jnp.logical_not(first))
        def _():
            hop(k, out_s, in_s, send, recv, target).wait_recv()
            got = in_s[sl]
            got_ref[sl] = got
            out_s[sl] = gam_ref[sl, :1, :] * got + own_ref[sl]

        @pl.when(jnp.logical_not(final))
        def _():
            hop(k, out_s, in_s, send, recv, target).start()

    right = jnp.minimum(mine + 1, last)
    left = jnp.maximum(mine - 1, 0)

    for b in range(nb):
        sl = slice(b * BLOCK, (b + 1) * BLOCK)
        ep = aux_ref[2, :8, sl]
        mask = (iota((BLOCK, BLOCK), 0) <= iota((BLOCK, BLOCK), 1)) & (
            jnp.abs(ep.T[:, :1] - ep[:1]) < 0.5
        )
        st_s[b] = jnp.where(mask, dot_nt(b_ref[sl, :], c_ref[sl, :]), 0.0)
    ds_ref[...] = jnp.zeros_like(ds_ref)

    def within_blocks(h):
        rows = rows_ref[h]
        cols = rows[: 2 * nb].T
        lanes = pl.ds(pl.multiple_of(h * width, width), width)
        for b in range(nb):
            sl = slice(b * BLOCK, (b + 1) * BLOCK)
            dy = dy_ref[sl, lanes]
            dmt = dot_nt(x_ref[sl, lanes], dy)
            decay = jnp.exp2(rows[b : b + 1] - cols[:, nb + b : nb + b + 1])
            mt = st_s[b] * decay
            ds_ref[b] += dmt * decay
            row_ref[pl.ds(h, 1), sl] = jnp.sum(dmt * mt, axis=0, keepdims=True)
            dxi_ref[sl, lanes] = dot(mt.astype(BF16), dy).astype(BF16)

    def tick(t, _):
        kf = t - mine * AHEAD
        kb = t - (last - mine) * AHEAD

        @pl.when((kf >= 0) & (kf < steps))
        def _():
            advance(kf, mine == 0, mine == last, right, local_ref, entry_ref, fout_s, fin_s, fsend, frecv)

        @pl.when((kb >= 0) & (kb < steps))
        def _():
            advance(kb, mine == last, mine == 0, left, back_ref, exit_ref, bout_s, bin_s, bsend, brecv)

        @pl.when(t < heads)
        def _():
            within_blocks(t)

        return 0

    lax.fori_loop(0, max(last * AHEAD + steps, heads), tick, 0)

    def drain(k, _):
        @pl.when(mine < last)
        def _():
            hop(k, fout_s, fin_s, fsend, frecv, right).wait_send()

        @pl.when(mine > 0)
        def _():
            hop(k, bout_s, bin_s, bsend, brecv, left).wait_send()

        return 0

    lax.fori_loop(0, steps, drain, 0)


def chain(gam, local, back, x, dy, b_proj, c_proj, rows, aux):
    heads = gam.shape[0]
    tokens = x.shape[0]
    pieces = jax.ShapeDtypeStruct((tokens // BLOCK, BLOCK, BLOCK), F32)
    steps = min(8, heads)
    spec = pl.BlockSpec(memory_space=pltpu.VMEM)
    out = jax.ShapeDtypeStruct(local.shape, F32)
    return pl.pallas_call(
        chain_kernel,
        in_specs=[spec] * 9,
        out_specs=[spec] * 5,
        out_shape=[
            out, out, jax.ShapeDtypeStruct(x.shape, BF16), pieces,
            jax.ShapeDtypeStruct((heads, tokens), F32),
        ],
        scratch_shapes=[pltpu.VMEM(pieces.shape, F32)] + [pltpu.VMEM(local.shape, F32)] * 4 + [pltpu.SemaphoreType.DMA((steps,))] * 4,
        compiler_params=pltpu.CompilerParams(
            collective_id=0, has_side_effects=True, vmem_limit_bytes=VMEM_LIMIT
        ),
    )(gam, local, back, x, dy, b_proj, c_proj, rows, aux)


def pair_kernel(gb_ref, gc_ref, ob_ref, oc_ref, got_b, got_c, send, recv):
    other = {"head": 1 - lax.axis_index("head")}
    barrier = pltpu.get_barrier_semaphore()
    pl.semaphore_signal(barrier, inc=1, device_id=other, device_id_type=MESH)
    pl.semaphore_wait(barrier, 1)
    pieces = send.shape[1]
    rows = gb_ref.shape[0] // pieces
    trio = ((gb_ref, got_b, ob_ref), (gc_ref, got_c, oc_ref))

    def hop(i, k):
        sl = slice(k * rows, (k + 1) * rows)
        return pltpu.make_async_remote_copy(
            src_ref=trio[i][0].at[sl], dst_ref=trio[i][1].at[sl], send_sem=send.at[i, k],
            recv_sem=recv.at[i, k], device_id=other, device_id_type=MESH,
        )

    copies = [(i, k, hop(i, k)) for i in range(2) for k in range(pieces)]
    for _, _, copy in copies:
        copy.start()
    for i, k, copy in copies:
        sl = slice(k * rows, (k + 1) * rows)
        copy.wait_recv()
        trio[i][2][sl] = trio[i][0][sl] + trio[i][1][sl]
    for _, _, copy in copies:
        copy.wait_send()


def over_heads(grad_b, grad_c):
    if lax.axis_size("head") != 2:
        return lax.psum((grad_b, grad_c), "head")
    spec = pl.BlockSpec(memory_space=pltpu.VMEM)
    out = jax.ShapeDtypeStruct(grad_b.shape, F32)
    return pl.pallas_call(
        pair_kernel,
        in_specs=[spec] * 2,
        out_specs=[spec] * 2,
        out_shape=[out, out],
        scratch_shapes=[pltpu.VMEM(grad_b.shape, F32)] * 2 + [pltpu.SemaphoreType.DMA((2, 4))] * 2,
        compiler_params=pltpu.CompilerParams(
            collective_id=1, has_side_effects=True, vmem_limit_bytes=VMEM_LIMIT
        ),
    )(grad_b, grad_c)


def on_device(
    activations, cotangent, b_proj, c_proj, dt_raw, resets, agents, agent_bias, a_log, d_skip
):
    heads = dt_raw.shape[0]
    width = activations.shape[1] // heads
    n = b_proj.shape[1]
    tokens = activations.shape[0]
    nb = tokens // BLOCK
    xspec = pl.BlockSpec((tokens, width), lambda h: (0, h))
    alog = a_log[:, None]
    sds = jax.ShapeDtypeStruct
    rows, aux, added, inject, local, back, gam = pl.pallas_call(
        partial(summary_kernel, nb),
        grid=(heads,),
        in_specs=[
            xspec, xspec, whole((tokens, n)), whole((tokens, n)), whole((heads, tokens)),
            whole((1, tokens)), whole((1, tokens)), whole(agent_bias.shape), whole((heads, 1)),
        ],
        out_specs=[
            whole((heads, 4 * nb, BLOCK)), whole((3, heads, tokens)), per_head((nb, n, width)),
            per_head((nb, n, width)), per_head((n, width)), per_head((n, width)), per_head((8, width)),
        ],
        out_shape=[
            sds((heads, 4 * nb, BLOCK), F32), sds((3, heads, tokens), F32),
            sds((heads, nb, n, width), F32), sds((heads, nb, n, width), BF16),
            sds((heads, n, width), F32), sds((heads, n, width), F32), sds((heads, 8, width), F32),
        ],
        scratch_shapes=[pltpu.VMEM((n, tokens), F32), pltpu.VMEM((n, tokens), F32)],
        compiler_params=pltpu.CompilerParams(vmem_limit_bytes=VMEM_LIMIT),
    )(
        activations, cotangent, b_proj, c_proj, dt_raw, resets[None], agents[None], agent_bias, alog
    )
    entry, exit_grad, dxi, ds, drow = chain(
        gam, local, back, activations, cotangent, b_proj, c_proj, rows, aux
    )
    grad_x, grad_b, grad_c, grad_rate = pl.pallas_call(
        partial(grad_kernel, nb),
        grid=(heads,),
        in_specs=[
            xspec, xspec, whole((tokens, n)), whole((tokens, n)), per_head((4 * nb, BLOCK)),
            whole((3, heads, tokens)), per_head((nb, n, width)), per_head((nb, n, width)),
            per_head((n, width)), per_head((n, width)), whole((heads, 1)),
            pl.BlockSpec(memory_space=pltpu.SMEM), xspec, whole((nb, BLOCK, BLOCK)),
            whole((heads, tokens)),
        ],
        out_specs=[xspec, whole((tokens, n)), whole((tokens, n)), whole((heads, tokens))],
        out_shape=[
            sds(activations.shape, BF16), sds((tokens, n), F32), sds((tokens, n), F32),
            sds((heads, tokens), F32),
        ],
        scratch_shapes=[
            pltpu.VMEM((n, tokens), F32), pltpu.VMEM((n, tokens), F32),
            pltpu.VMEM((n, tokens), F32), pltpu.VMEM((n, tokens), F32),
            pltpu.VMEM((heads, tokens), F32), pltpu.VMEM((heads, tokens), F32),
        ],
        compiler_params=pltpu.CompilerParams(vmem_limit_bytes=VMEM_LIMIT),
    )(
        activations, cotangent, b_proj, c_proj, rows, aux, added, inject, entry, exit_grad, alog,
        d_skip, dxi, ds, drow,
    )
    grad_b, grad_c = over_heads(grad_b, grad_c)
    return (grad_x, grad_b, grad_c, grad_rate)


def solution(mesh):
    tok = ("grp", "seq", "rep")
    return jax.shard_map(
        on_device,
        mesh=mesh,
        in_specs=(
            P(tok, "head"), P(tok, "head"), P(tok, None), P(tok, None), P("head", tok),
            P(tok), P(tok), P("head", None), P("head"), P("head"),
        ),
        out_specs=(P(tok, "head"), P(tok, None), P(tok, None), P("head", tok)),
        check_vma=False,
    )
```

```python
from functools import partial

import jax
import jax.numpy as jnp
from jax import lax
from jax.experimental import pallas as pl
from jax.experimental.pallas import tpu as pltpu
from jax.sharding import PartitionSpec as P

BLOCK = 256
LOG2E = 1.4426950408889634
HI = lax.Precision.HIGHEST
F32 = jnp.float32
BF16 = jnp.bfloat16
NT = (((1,), (1,)), ((), ()))
VMEM_LIMIT = 62 * 1024 * 1024


def dot(a, b):
    return jnp.dot(a, b, preferred_element_type=F32)


def dot_nt(a, b):
    return lax.dot_general(a, b, NT, preferred_element_type=F32)


def dot_hi(a, b):
    return jnp.dot(a, b, precision=HI, preferred_element_type=F32)


def iota(shape, axis):
    return lax.broadcasted_iota(jnp.int32, shape, axis)


def summary_kernel(
    nb, x_ref, dy_ref, b_ref, c_ref, raw_ref, res_ref, ag_ref, bias_ref, alog_ref,
    rows_ref, aux_ref, added_ref, inject_ref, local_ref, back_ref, gam_ref, bt_s, ct_s,
):
    h = pl.program_id(0)
    heads = raw_ref.shape[0]

    @pl.when(h == 0)
    def _():
        upper = (iota((BLOCK, BLOCK), 0) <= iota((BLOCK, BLOCK), 1)).astype(F32)
        rate = jnp.exp(alog_ref[...])
        for b in range(nb):
            sl = slice(b * BLOCK, (b + 1) * BLOCK)
            bt_s[:, sl] = b_ref[sl, :].astype(F32).T
            ct_s[:, sl] = c_ref[sl, :].astype(F32).T
            onehot = (ag_ref[:, sl] == iota((bias_ref.shape[1], BLOCK), 0)).astype(F32)
            v = raw_ref[:, sl] + dot_hi(bias_ref[...], onehot)
            ev = jnp.exp(v)
            s = jnp.where(v > 15.0, v, jnp.log1p(ev))
            log_decay = -rate * s
            cum = dot_hi(log_decay, upper)
            res = jnp.broadcast_to(res_ref[:, sl].astype(F32), (8, BLOCK))
            ep = dot_hi(res, upper)[:1]
            cum2 = cum * LOG2E
            entry = jnp.where(ep < 0.5, jnp.exp(cum), 0.0)
            last = cum[:, BLOCK - 1 :]
            to_end = jnp.where(jnp.abs(ep - ep[:, BLOCK - 1 :]) < 0.5, jnp.exp(last - cum) * s, 0.0)
            rows_ref[:, b, :] = cum2
            rows_ref[:, nb + b, :] = cum2 - jnp.log2(s)
            rows_ref[:, 2 * nb + b, :] = entry
            rows_ref[:, 3 * nb + b, :] = to_end
            aux_ref[0, :, sl] = 1.0 / s
            aux_ref[1, :, sl] = ev / (1.0 + ev)
            aux_ref[2, :, sl] = jnp.broadcast_to(ep, (heads, BLOCK))

    added, inject, gammas = [], [], []
    for b in range(nb):
        sl = slice(b * BLOCK, (b + 1) * BLOCK)
        e_row = rows_ref[h, pl.ds(2 * nb + b, 1), :]
        t_row = rows_ref[h, pl.ds(3 * nb + b, 1), :]
        add = dot((bt_s[:, sl] * t_row).astype(BF16), x_ref[sl, :])
        inj = dot((ct_s[:, sl] * e_row).astype(BF16), dy_ref[sl, :]).astype(BF16)
        added_ref[0, b] = add
        inject_ref[0, b] = inj
        added.append(add)
        inject.append(inj.astype(F32))
        gammas.append(e_row[:, BLOCK - 1 :])
    local, back, total = added[0], inject[nb - 1], gammas[0]
    for b in range(1, nb):
        local = gammas[b] * local + added[b]
        total = total * gammas[b]
        back = gammas[nb - 1 - b] * back + inject[nb - 1 - b]
    local_ref[0] = local
    back_ref[0] = back
    gam_ref[0] = jnp.broadcast_to(total, gam_ref.shape[1:])


def grad_kernel(
    nb, x_ref, dy_ref, b_ref, c_ref, rows_ref, aux_ref, added_ref, inject_ref,
    entry_ref, exit_ref, alog_ref, dskip_ref,
    gx_ref, gb_ref, gc_ref, gr_ref,
    bt_s, ct_s, st_s, ds_s, dbt_s, dct_s, drow_s, dcol_s,
):
    h = pl.program_id(0)

    @pl.when(h == 0)
    def _():
        for b in range(nb):
            sl = slice(b * BLOCK, (b + 1) * BLOCK)
            bt_s[:, sl] = b_ref[sl, :].astype(F32).T
            ct_s[:, sl] = c_ref[sl, :].astype(F32).T
            ep = aux_ref[2, :8, sl]
            ep_col = ep.T[:, :1]
            mask = (iota((BLOCK, BLOCK), 0) <= iota((BLOCK, BLOCK), 1)) & (
                jnp.abs(ep_col - ep[:1]) < 0.5
            )
            st_s[b] = jnp.where(mask, dot_nt(b_ref[sl, :], c_ref[sl, :]), 0.0)
        ds_s[...] = jnp.zeros_like(ds_s)
        dbt_s[...] = jnp.zeros_like(dbt_s)
        dct_s[...] = jnp.zeros_like(dct_s)

    rows = rows_ref[0]
    cols = rows.T
    ones = jnp.ones((8, x_ref.shape[1]), BF16)
    d_h = dskip_ref[h]
    gam = [rows[2 * nb + b : 2 * nb + b + 1, BLOCK - 1 :] for b in range(nb)]
    states = [entry_ref[0]]
    for b in range(nb):
        states.append(gam[b] * states[b] + added_ref[0, b])
    grads = [exit_ref[0]]
    for b in range(nb - 1, 0, -1):
        grads.insert(0, gam[b] * grads[0] + inject_ref[0, b].astype(F32))
    for b in range(nb):
        sl = slice(b * BLOCK, (b + 1) * BLOCK)
        x, dy = x_ref[sl, :], dy_ref[sl, :]
        g16 = grads[b].astype(BF16)
        s16 = states[b].astype(BF16)
        dmt = dot_nt(x, dy)
        decay = jnp.exp2(rows[b : b + 1] - cols[:, nb + b : nb + b + 1])
        mt = st_s[b] * decay
        ds_s[b] += dmt * decay
        row = jnp.sum(dmt * mt, axis=0, keepdims=True)
        dcs = dot_nt(s16, dy) * rows[2 * nb + b : 2 * nb + b + 1]
        dct_s[:, sl] += dcs
        row += jnp.sum(dcs * ct_s[:, sl], axis=0, keepdims=True)
        row_end = jnp.sum(jnp.sum(grads[b] * states[b + 1], axis=0, keepdims=True), axis=1, keepdims=True)
        dbt_s[:, sl] += dot_nt(g16, x) * rows[3 * nb + b : 3 * nb + b + 1]
        dx = dot(mt.astype(BF16), dy) + cols[:, 3 * nb + b : 3 * nb + b + 1] * dot(b_ref[sl, :], g16)
        z = x.astype(F32) * dx
        zh = z.astype(BF16)
        zl = (z - zh.astype(F32)).astype(BF16)
        col = (dot_nt(ones, zh) + dot_nt(ones, zl))[:1]
        gx_ref[sl, :] = (dx + d_h * dy.astype(F32)).astype(BF16)
        last = iota((1, BLOCK), 1) == BLOCK - 1
        drow_s[pl.ds(h, 1), sl] = row - col + jnp.where(last, row_end, 0.0)
        dcol_s[pl.ds(h, 1), sl] = col

    @pl.when(h == pl.num_programs(0) - 1)
    def _():
        lower = (iota((BLOCK, BLOCK), 0) >= iota((BLOCK, BLOCK), 1)).astype(F32)
        rate = jnp.exp(alog_ref[...])
        for b in range(nb):
            sl = slice(b * BLOCK, (b + 1) * BLOCK)
            dlog = dot_hi(drow_s[:, sl], lower)
            gr_ref[:, sl] = (dcol_s[:, sl] * aux_ref[0, :, sl] - rate * dlog) * aux_ref[1, :, sl]
            ep = aux_ref[2, :8, sl]
            ep_col = ep.T[:, :1]
            mask = (iota((BLOCK, BLOCK), 0) <= iota((BLOCK, BLOCK), 1)) & (
                jnp.abs(ep_col - ep[:1]) < 0.5
            )
            ds = jnp.where(mask, ds_s[b], 0.0)
            dh = ds.astype(BF16)
            dl = (ds - dh.astype(F32)).astype(BF16)
            ct = ct_s[:, sl].astype(BF16)
            bt = bt_s[:, sl].astype(BF16)
            gb_ref[sl, :] = (dbt_s[:, sl] + dot_nt(ct, dh) + dot_nt(ct, dl)).T
            gc_ref[sl, :] = (dct_s[:, sl] + dot(bt, dh) + dot(bt, dl)).T


def whole(shape):
    return pl.BlockSpec(shape, lambda h: (0,) * len(shape))


def per_head(shape):
    return pl.BlockSpec((1,) + shape, lambda h: (h,) + (0,) * len(shape))


MESH = pl.DeviceIdType.MESH
AHEAD = 4


def chain_kernel(
    gam_ref, local_ref, back_ref, entry_ref, exit_ref,
    fin_s, fout_s, bin_s, bout_s, fsend, frecv, bsend, brecv,
):
    reps = lax.axis_size("rep")
    last = lax.axis_size("seq") * reps - 1
    mine = lax.axis_index("seq") * reps + lax.axis_index("rep")
    steps = fsend.shape[0]
    per = gam_ref.shape[0] // steps

    def place(index):
        return {"seq": index // reps, "rep": index % reps}

    barrier = pltpu.get_barrier_semaphore()

    @pl.when(mine > 0)
    def _():
        pl.semaphore_signal(barrier, inc=1, device_id=place(mine - 1), device_id_type=MESH)

    @pl.when(mine < last)
    def _():
        pl.semaphore_signal(barrier, inc=1, device_id=place(mine + 1), device_id_type=MESH)

    edge = (mine == 0) | (mine == last)

    @pl.when(edge)
    def _():
        pl.semaphore_wait(barrier, 1)

    @pl.when(jnp.logical_not(edge))
    def _():
        pl.semaphore_wait(barrier, 2)

    def hop(k, out_s, in_s, send, recv, target):
        sl = pl.ds(k * per, per)
        return pltpu.make_async_remote_copy(
            src_ref=out_s.at[sl], dst_ref=in_s.at[sl], send_sem=send.at[k], recv_sem=recv.at[k],
            device_id=place(target), device_id_type=MESH,
        )

    def advance(k, first, final, target, own_ref, got_ref, out_s, in_s, send, recv):
        sl = pl.ds(k * per, per)

        @pl.when(first)
        def _():
            got_ref[sl] = jnp.zeros_like(got_ref[sl])
            out_s[sl] = own_ref[sl]

        @pl.when(jnp.logical_not(first))
        def _():
            hop(k, out_s, in_s, send, recv, target).wait_recv()
            got = in_s[sl]
            got_ref[sl] = got
            out_s[sl] = gam_ref[sl, :1, :] * got + own_ref[sl]

        @pl.when(jnp.logical_not(final))
        def _():
            hop(k, out_s, in_s, send, recv, target).start()

    right = jnp.minimum(mine + 1, last)
    left = jnp.maximum(mine - 1, 0)

    def tick(t, _):
        kf = t - mine * AHEAD
        kb = t - (last - mine) * AHEAD

        @pl.when((kf >= 0) & (kf < steps))
        def _():
            advance(kf, mine == 0, mine == last, right, local_ref, entry_ref, fout_s, fin_s, fsend, frecv)

        @pl.when((kb >= 0) & (kb < steps))
        def _():
            advance(kb, mine == last, mine == 0, left, back_ref, exit_ref, bout_s, bin_s, bsend, brecv)

        return 0

    lax.fori_loop(0, last * AHEAD + steps, tick, 0)

    def drain(k, _):
        @pl.when(mine < last)
        def _():
            hop(k, fout_s, fin_s, fsend, frecv, right).wait_send()

        @pl.when(mine > 0)
        def _():
            hop(k, bout_s, bin_s, bsend, brecv, left).wait_send()

        return 0

    lax.fori_loop(0, steps, drain, 0)


def chain(gam, local, back):
    heads = gam.shape[0]
    steps = heads
    spec = pl.BlockSpec(memory_space=pltpu.VMEM)
    out = jax.ShapeDtypeStruct(local.shape, F32)
    return pl.pallas_call(
        chain_kernel,
        in_specs=[spec] * 3,
        out_specs=[spec] * 2,
        out_shape=[out, out],
        scratch_shapes=[pltpu.VMEM(local.shape, F32)] * 4 + [pltpu.SemaphoreType.DMA((steps,))] * 4,
        compiler_params=pltpu.CompilerParams(
            collective_id=0, has_side_effects=True, vmem_limit_bytes=VMEM_LIMIT
        ),
    )(gam, local, back)


def pair_kernel(gb_ref, gc_ref, ob_ref, oc_ref, got_b, got_c, send, recv):
    other = {"head": 1 - lax.axis_index("head")}
    barrier = pltpu.get_barrier_semaphore()
    pl.semaphore_signal(barrier, inc=1, device_id=other, device_id_type=MESH)
    pl.semaphore_wait(barrier, 1)
    pieces = send.shape[1]
    rows = gb_ref.shape[0] // pieces
    trio = ((gb_ref, got_b, ob_ref), (gc_ref, got_c, oc_ref))

    def hop(i, k):
        sl = slice(k * rows, (k + 1) * rows)
        return pltpu.make_async_remote_copy(
            src_ref=trio[i][0].at[sl], dst_ref=trio[i][1].at[sl], send_sem=send.at[i, k],
            recv_sem=recv.at[i, k], device_id=other, device_id_type=MESH,
        )

    copies = [(i, k, hop(i, k)) for i in range(2) for k in range(pieces)]
    for _, _, copy in copies:
        copy.start()
    for i, k, copy in copies:
        sl = slice(k * rows, (k + 1) * rows)
        copy.wait_recv()
        trio[i][2][sl] = trio[i][0][sl] + trio[i][1][sl]
    for _, _, copy in copies:
        copy.wait_send()


def over_heads(grad_b, grad_c):
    if lax.axis_size("head") != 2:
        return lax.psum((grad_b, grad_c), "head")
    spec = pl.BlockSpec(memory_space=pltpu.VMEM)
    out = jax.ShapeDtypeStruct(grad_b.shape, F32)
    return pl.pallas_call(
        pair_kernel,
        in_specs=[spec] * 2,
        out_specs=[spec] * 2,
        out_shape=[out, out],
        scratch_shapes=[pltpu.VMEM(grad_b.shape, F32)] * 2 + [pltpu.SemaphoreType.DMA((2, 4))] * 2,
        compiler_params=pltpu.CompilerParams(
            collective_id=1, has_side_effects=True, vmem_limit_bytes=VMEM_LIMIT
        ),
    )(grad_b, grad_c)


def on_device(
    activations, cotangent, b_proj, c_proj, dt_raw, resets, agents, agent_bias, a_log, d_skip
):
    heads = dt_raw.shape[0]
    width = activations.shape[1] // heads
    n = b_proj.shape[1]
    tokens = activations.shape[0]
    nb = tokens // BLOCK
    xspec = pl.BlockSpec((tokens, width), lambda h: (0, h))
    alog = a_log[:, None]
    sds = jax.ShapeDtypeStruct
    rows, aux, added, inject, local, back, gam = pl.pallas_call(
        partial(summary_kernel, nb),
        grid=(heads,),
        in_specs=[
            xspec, xspec, whole((tokens, n)), whole((tokens, n)), whole((heads, tokens)),
            whole((1, tokens)), whole((1, tokens)), whole(agent_bias.shape), whole((heads, 1)),
        ],
        out_specs=[
            whole((heads, 4 * nb, BLOCK)), whole((3, heads, tokens)), per_head((nb, n, width)),
            per_head((nb, n, width)), per_head((n, width)), per_head((n, width)), per_head((8, width)),
        ],
        out_shape=[
            sds((heads, 4 * nb, BLOCK), F32), sds((3, heads, tokens), F32),
            sds((heads, nb, n, width), F32), sds((heads, nb, n, width), BF16),
            sds((heads, n, width), F32), sds((heads, n, width), F32), sds((heads, 8, width), F32),
        ],
        scratch_shapes=[pltpu.VMEM((n, tokens), F32), pltpu.VMEM((n, tokens), F32)],
        compiler_params=pltpu.CompilerParams(vmem_limit_bytes=VMEM_LIMIT),
    )(
        activations, cotangent, b_proj, c_proj, dt_raw, resets[None], agents[None], agent_bias, alog
    )
    entry, exit_grad = chain(gam, local, back)
    grad_x, grad_b, grad_c, grad_rate = pl.pallas_call(
        partial(grad_kernel, nb),
        grid=(heads,),
        in_specs=[
            xspec, xspec, whole((tokens, n)), whole((tokens, n)), per_head((4 * nb, BLOCK)),
            whole((3, heads, tokens)), per_head((nb, n, width)), per_head((nb, n, width)),
            per_head((n, width)), per_head((n, width)), whole((heads, 1)),
            pl.BlockSpec(memory_space=pltpu.SMEM),
        ],
        out_specs=[xspec, whole((tokens, n)), whole((tokens, n)), whole((heads, tokens))],
        out_shape=[
            sds(activations.shape, BF16), sds((tokens, n), F32), sds((tokens, n), F32),
            sds((heads, tokens), F32),
        ],
        scratch_shapes=[
            pltpu.VMEM((n, tokens), F32), pltpu.VMEM((n, tokens), F32),
            pltpu.VMEM((nb, BLOCK, BLOCK), F32), pltpu.VMEM((nb, BLOCK, BLOCK), F32),
            pltpu.VMEM((n, tokens), F32), pltpu.VMEM((n, tokens), F32),
            pltpu.VMEM((heads, tokens), F32), pltpu.VMEM((heads, tokens), F32),
        ],
        compiler_params=pltpu.CompilerParams(vmem_limit_bytes=VMEM_LIMIT),
    )(
        activations, cotangent, b_proj, c_proj, rows, aux, added, inject, entry, exit_grad, alog,
        d_skip,
    )
    grad_b, grad_c = over_heads(grad_b, grad_c)
    return (grad_x, grad_b, grad_c, grad_rate)


def solution(mesh):
    tok = ("grp", "seq", "rep")
    return jax.shard_map(
        on_device,
        mesh=mesh,
        in_specs=(
            P(tok, "head"), P(tok, "head"), P(tok, None), P(tok, None), P("head", tok),
            P(tok), P(tok), P("head", None), P("head"), P("head"),
        ),
        out_specs=(P(tok, "head"), P(tok, None), P(tok, None), P("head", tok)),
        check_vma=False,
    )
```

```python
from functools import partial

import jax
import jax.numpy as jnp
from jax import lax
from jax.experimental import pallas as pl
from jax.experimental.pallas import tpu as pltpu
from jax.sharding import PartitionSpec as P

BLOCK = 256
LOG2E = 1.4426950408889634
HI = lax.Precision.HIGHEST
F32 = jnp.float32
BF16 = jnp.bfloat16
NT = (((1,), (1,)), ((), ()))
VMEM_LIMIT = 50 * 1024 * 1024


def dot(a, b):
    return jnp.dot(a, b, preferred_element_type=F32)


def dot_nt(a, b):
    return lax.dot_general(a, b, NT, preferred_element_type=F32)


def dot_hi(a, b):
    return jnp.dot(a, b, precision=HI, preferred_element_type=F32)


def iota(shape, axis):
    return lax.broadcasted_iota(jnp.int32, shape, axis)


def summary_kernel(
    nb, x_ref, dy_ref, b_ref, c_ref, raw_ref, res_ref, ag_ref, bias_ref, alog_ref,
    rows_ref, aux_ref, added_ref, inject_ref, local_ref, back_ref, gam_ref, bt_s, ct_s,
):
    h = pl.program_id(0)
    heads = raw_ref.shape[0]

    @pl.when(h == 0)
    def _():
        upper = (iota((BLOCK, BLOCK), 0) <= iota((BLOCK, BLOCK), 1)).astype(F32)
        rate = jnp.exp(alog_ref[...])
        for b in range(nb):
            sl = slice(b * BLOCK, (b + 1) * BLOCK)
            bt_s[:, sl] = b_ref[sl, :].astype(F32).T
            ct_s[:, sl] = c_ref[sl, :].astype(F32).T
            onehot = (ag_ref[:, sl] == iota((bias_ref.shape[1], BLOCK), 0)).astype(F32)
            v = raw_ref[:, sl] + dot_hi(bias_ref[...], onehot)
            ev = jnp.exp(v)
            s = jnp.where(v > 15.0, v, jnp.log1p(ev))
            log_decay = -rate * s
            cum = dot_hi(log_decay, upper)
            res = jnp.broadcast_to(res_ref[:, sl].astype(F32), (8, BLOCK))
            ep = dot_hi(res, upper)[:1]
            cum2 = cum * LOG2E
            entry = jnp.where(ep < 0.5, jnp.exp(cum), 0.0)
            last = cum[:, BLOCK - 1 :]
            to_end = jnp.where(jnp.abs(ep - ep[:, BLOCK - 1 :]) < 0.5, jnp.exp(last - cum) * s, 0.0)
            rows_ref[:, b, :] = cum2
            rows_ref[:, nb + b, :] = cum2 - jnp.log2(s)
            rows_ref[:, 2 * nb + b, :] = entry
            rows_ref[:, 3 * nb + b, :] = to_end
            aux_ref[0, :, sl] = 1.0 / s
            aux_ref[1, :, sl] = ev / (1.0 + ev)
            aux_ref[2, :, sl] = jnp.broadcast_to(ep, (heads, BLOCK))

    added, inject, gammas = [], [], []
    for b in range(nb):
        sl = slice(b * BLOCK, (b + 1) * BLOCK)
        e_row = rows_ref[h, pl.ds(2 * nb + b, 1), :]
        t_row = rows_ref[h, pl.ds(3 * nb + b, 1), :]
        add = dot((bt_s[:, sl] * t_row).astype(BF16), x_ref[sl, :])
        inj = dot((ct_s[:, sl] * e_row).astype(BF16), dy_ref[sl, :]).astype(BF16)
        added_ref[0, b] = add
        inject_ref[0, b] = inj
        added.append(add)
        inject.append(inj.astype(F32))
        gammas.append(e_row[:, BLOCK - 1 :])
    local, back, total = added[0], inject[nb - 1], gammas[0]
    for b in range(1, nb):
        local = gammas[b] * local + added[b]
        total = total * gammas[b]
        back = gammas[nb - 1 - b] * back + inject[nb - 1 - b]
    local_ref[0] = local
    back_ref[0] = back
    gam_ref[0] = jnp.broadcast_to(total, gam_ref.shape[1:])


def grad_kernel(
    nb, x_ref, dy_ref, b_ref, c_ref, rows_ref, aux_ref, added_ref, inject_ref,
    entry_ref, exit_ref, alog_ref, dskip_ref,
    gx_ref, gb_ref, gc_ref, gr_ref,
    bt_s, ct_s, st_s, ds_s, dbt_s, dct_s, drow_s, dcol_s,
):
    h = pl.program_id(0)

    @pl.when(h == 0)
    def _():
        for b in range(nb):
            sl = slice(b * BLOCK, (b + 1) * BLOCK)
            bt_s[:, sl] = b_ref[sl, :].astype(F32).T
            ct_s[:, sl] = c_ref[sl, :].astype(F32).T
            ep = aux_ref[2, :8, sl]
            ep_col = ep.T[:, :1]
            mask = (iota((BLOCK, BLOCK), 0) <= iota((BLOCK, BLOCK), 1)) & (
                jnp.abs(ep_col - ep[:1]) < 0.5
            )
            st_s[b] = jnp.where(mask, dot_nt(b_ref[sl, :], c_ref[sl, :]), 0.0)
        ds_s[...] = jnp.zeros_like(ds_s)
        dbt_s[...] = jnp.zeros_like(dbt_s)
        dct_s[...] = jnp.zeros_like(dct_s)

    rows = rows_ref[0]
    cols = rows.T
    ones = jnp.ones((8, x_ref.shape[1]), BF16)
    d_h = dskip_ref[h]
    gam = [rows[2 * nb + b : 2 * nb + b + 1, BLOCK - 1 :] for b in range(nb)]
    states = [entry_ref[0]]
    for b in range(nb):
        states.append(gam[b] * states[b] + added_ref[0, b])
    grads = [exit_ref[0]]
    for b in range(nb - 1, 0, -1):
        grads.insert(0, gam[b] * grads[0] + inject_ref[0, b].astype(F32))
    for b in range(nb):
        sl = slice(b * BLOCK, (b + 1) * BLOCK)
        x, dy = x_ref[sl, :], dy_ref[sl, :]
        g16 = grads[b].astype(BF16)
        s16 = states[b].astype(BF16)
        dmt = dot_nt(x, dy)
        decay = jnp.exp2(rows[b : b + 1] - cols[:, nb + b : nb + b + 1])
        mt = st_s[b] * decay
        ds_s[b] += dmt * decay
        row = jnp.sum(dmt * mt, axis=0, keepdims=True)
        dcs = dot_nt(s16, dy) * rows[2 * nb + b : 2 * nb + b + 1]
        dct_s[:, sl] += dcs
        row += jnp.sum(dcs * ct_s[:, sl], axis=0, keepdims=True)
        row_end = jnp.sum(jnp.sum(grads[b] * states[b + 1], axis=0, keepdims=True), axis=1, keepdims=True)
        dbt_s[:, sl] += dot_nt(g16, x) * rows[3 * nb + b : 3 * nb + b + 1]
        dx = dot(mt.astype(BF16), dy) + cols[:, 3 * nb + b : 3 * nb + b + 1] * dot(b_ref[sl, :], g16)
        z = x.astype(F32) * dx
        col = dot_nt(ones, z.astype(BF16))[:1]
        gx_ref[sl, :] = (dx + d_h * dy.astype(F32)).astype(BF16)
        last = iota((1, BLOCK), 1) == BLOCK - 1
        drow_s[pl.ds(h, 1), sl] = row - col + jnp.where(last, row_end, 0.0)
        dcol_s[pl.ds(h, 1), sl] = col

    @pl.when(h == pl.num_programs(0) - 1)
    def _():
        lower = (iota((BLOCK, BLOCK), 0) >= iota((BLOCK, BLOCK), 1)).astype(F32)
        rate = jnp.exp(alog_ref[...])
        for b in range(nb):
            sl = slice(b * BLOCK, (b + 1) * BLOCK)
            dlog = dot_hi(drow_s[:, sl], lower)
            gr_ref[:, sl] = (dcol_s[:, sl] * aux_ref[0, :, sl] - rate * dlog) * aux_ref[1, :, sl]
            ep = aux_ref[2, :8, sl]
            ep_col = ep.T[:, :1]
            mask = (iota((BLOCK, BLOCK), 0) <= iota((BLOCK, BLOCK), 1)) & (
                jnp.abs(ep_col - ep[:1]) < 0.5
            )
            ds = jnp.where(mask, ds_s[b], 0.0)
            dh = ds.astype(BF16)
            dl = (ds - dh.astype(F32)).astype(BF16)
            ct = ct_s[:, sl].astype(BF16)
            bt = bt_s[:, sl].astype(BF16)
            gb_ref[sl, :] = (dbt_s[:, sl] + dot_nt(ct, dh) + dot_nt(ct, dl)).T
            gc_ref[sl, :] = (dct_s[:, sl] + dot(bt, dh) + dot(bt, dl)).T


def whole(shape):
    return pl.BlockSpec(shape, lambda h: (0,) * len(shape))


def per_head(shape):
    return pl.BlockSpec((1,) + shape, lambda h: (h,) + (0,) * len(shape))


MESH = pl.DeviceIdType.MESH
AHEAD = 2


def chain_kernel(
    gam_ref, local_ref, back_ref, entry_ref, exit_ref,
    fin_s, fout_s, bin_s, bout_s, fsend, frecv, bsend, brecv,
):
    reps = lax.axis_size("rep")
    last = lax.axis_size("seq") * reps - 1
    mine = lax.axis_index("seq") * reps + lax.axis_index("rep")
    steps = fsend.shape[0]
    per = gam_ref.shape[0] // steps

    def place(index):
        return {"seq": index // reps, "rep": index % reps}

    barrier = pltpu.get_barrier_semaphore()

    @pl.when(mine > 0)
    def _():
        pl.semaphore_signal(barrier, inc=1, device_id=place(mine - 1), device_id_type=MESH)

    @pl.when(mine < last)
    def _():
        pl.semaphore_signal(barrier, inc=1, device_id=place(mine + 1), device_id_type=MESH)

    edge = (mine == 0) | (mine == last)

    @pl.when(edge)
    def _():
        pl.semaphore_wait(barrier, 1)

    @pl.when(jnp.logical_not(edge))
    def _():
        pl.semaphore_wait(barrier, 2)

    def hop(k, out_s, in_s, send, recv, target):
        sl = pl.ds(k * per, per)
        return pltpu.make_async_remote_copy(
            src_ref=out_s.at[sl], dst_ref=in_s.at[sl], send_sem=send.at[k], recv_sem=recv.at[k],
            device_id=place(target), device_id_type=MESH,
        )

    def advance(k, first, final, target, own_ref, got_ref, out_s, in_s, send, recv):
        sl = pl.ds(k * per, per)

        @pl.when(first)
        def _():
            got_ref[sl] = jnp.zeros_like(got_ref[sl])
            out_s[sl] = own_ref[sl]

        @pl.when(jnp.logical_not(first))
        def _():
            hop(k, out_s, in_s, send, recv, target).wait_recv()
            got = in_s[sl]
            got_ref[sl] = got
            out_s[sl] = gam_ref[sl, :1, :] * got + own_ref[sl]

        @pl.when(jnp.logical_not(final))
        def _():
            hop(k, out_s, in_s, send, recv, target).start()

    right = jnp.minimum(mine + 1, last)
    left = jnp.maximum(mine - 1, 0)

    def tick(t, _):
        kf = t - mine * AHEAD
        kb = t - (last - mine) * AHEAD

        @pl.when((kf >= 0) & (kf < steps))
        def _():
            advance(kf, mine == 0, mine == last, right, local_ref, entry_ref, fout_s, fin_s, fsend, frecv)

        @pl.when((kb >= 0) & (kb < steps))
        def _():
            advance(kb, mine == last, mine == 0, left, back_ref, exit_ref, bout_s, bin_s, bsend, brecv)

        return 0

    lax.fori_loop(0, last * AHEAD + steps, tick, 0)

    def drain(k, _):
        @pl.when(mine < last)
        def _():
            hop(k, fout_s, fin_s, fsend, frecv, right).wait_send()

        @pl.when(mine > 0)
        def _():
            hop(k, bout_s, bin_s, bsend, brecv, left).wait_send()

        return 0

    lax.fori_loop(0, steps, drain, 0)


def chain(gam, local, back):
    heads = gam.shape[0]
    steps = min(8, heads)
    spec = pl.BlockSpec(memory_space=pltpu.VMEM)
    out = jax.ShapeDtypeStruct(local.shape, F32)
    return pl.pallas_call(
        chain_kernel,
        in_specs=[spec] * 3,
        out_specs=[spec] * 2,
        out_shape=[out, out],
        scratch_shapes=[pltpu.VMEM(local.shape, F32)] * 4 + [pltpu.SemaphoreType.DMA((steps,))] * 4,
        compiler_params=pltpu.CompilerParams(
            collective_id=0, has_side_effects=True, vmem_limit_bytes=VMEM_LIMIT
        ),
    )(gam, local, back)


def pair_kernel(gb_ref, gc_ref, ob_ref, oc_ref, got_b, got_c, send, recv):
    other = {"head": 1 - lax.axis_index("head")}
    barrier = pltpu.get_barrier_semaphore()
    pl.semaphore_signal(barrier, inc=1, device_id=other, device_id_type=MESH)
    pl.semaphore_wait(barrier, 1)
    pieces = send.shape[1]
    rows = gb_ref.shape[0] // pieces
    trio = ((gb_ref, got_b, ob_ref), (gc_ref, got_c, oc_ref))

    def hop(i, k):
        sl = slice(k * rows, (k + 1) * rows)
        return pltpu.make_async_remote_copy(
            src_ref=trio[i][0].at[sl], dst_ref=trio[i][1].at[sl], send_sem=send.at[i, k],
            recv_sem=recv.at[i, k], device_id=other, device_id_type=MESH,
        )

    copies = [(i, k, hop(i, k)) for i in range(2) for k in range(pieces)]
    for _, _, copy in copies:
        copy.start()
    for i, k, copy in copies:
        sl = slice(k * rows, (k + 1) * rows)
        copy.wait_recv()
        trio[i][2][sl] = trio[i][0][sl] + trio[i][1][sl]
    for _, _, copy in copies:
        copy.wait_send()


def over_heads(grad_b, grad_c):
    if lax.axis_size("head") != 2:
        return lax.psum((grad_b, grad_c), "head")
    spec = pl.BlockSpec(memory_space=pltpu.VMEM)
    out = jax.ShapeDtypeStruct(grad_b.shape, F32)
    return pl.pallas_call(
        pair_kernel,
        in_specs=[spec] * 2,
        out_specs=[spec] * 2,
        out_shape=[out, out],
        scratch_shapes=[pltpu.VMEM(grad_b.shape, F32)] * 2 + [pltpu.SemaphoreType.DMA((2, 4))] * 2,
        compiler_params=pltpu.CompilerParams(
            collective_id=1, has_side_effects=True, vmem_limit_bytes=VMEM_LIMIT
        ),
    )(grad_b, grad_c)


def on_device(
    activations, cotangent, b_proj, c_proj, dt_raw, resets, agents, agent_bias, a_log, d_skip
):
    heads = dt_raw.shape[0]
    width = activations.shape[1] // heads
    n = b_proj.shape[1]
    tokens = activations.shape[0]
    nb = tokens // BLOCK
    xspec = pl.BlockSpec((tokens, width), lambda h: (0, h))
    alog = a_log[:, None]
    sds = jax.ShapeDtypeStruct
    rows, aux, added, inject, local, back, gam = pl.pallas_call(
        partial(summary_kernel, nb),
        grid=(heads,),
        in_specs=[
            xspec, xspec, whole((tokens, n)), whole((tokens, n)), whole((heads, tokens)),
            whole((1, tokens)), whole((1, tokens)), whole(agent_bias.shape), whole((heads, 1)),
        ],
        out_specs=[
            whole((heads, 4 * nb, BLOCK)), whole((3, heads, tokens)), per_head((nb, n, width)),
            per_head((nb, n, width)), per_head((n, width)), per_head((n, width)), per_head((8, width)),
        ],
        out_shape=[
            sds((heads, 4 * nb, BLOCK), F32), sds((3, heads, tokens), F32),
            sds((heads, nb, n, width), F32), sds((heads, nb, n, width), BF16),
            sds((heads, n, width), F32), sds((heads, n, width), F32), sds((heads, 8, width), F32),
        ],
        scratch_shapes=[pltpu.VMEM((n, tokens), F32), pltpu.VMEM((n, tokens), F32)],
        compiler_params=pltpu.CompilerParams(vmem_limit_bytes=62 * 1024 * 1024),
    )(
        activations, cotangent, b_proj, c_proj, dt_raw, resets[None], agents[None], agent_bias, alog
    )
    entry, exit_grad = chain(gam, local, back)
    grad_x, grad_b, grad_c, grad_rate = pl.pallas_call(
        partial(grad_kernel, nb),
        grid=(heads,),
        in_specs=[
            xspec, xspec, whole((tokens, n)), whole((tokens, n)), per_head((4 * nb, BLOCK)),
            whole((3, heads, tokens)), per_head((nb, n, width)), per_head((nb, n, width)),
            per_head((n, width)), per_head((n, width)), whole((heads, 1)),
            pl.BlockSpec(memory_space=pltpu.SMEM),
        ],
        out_specs=[xspec, whole((tokens, n)), whole((tokens, n)), whole((heads, tokens))],
        out_shape=[
            sds(activations.shape, BF16), sds((tokens, n), F32), sds((tokens, n), F32),
            sds((heads, tokens), F32),
        ],
        scratch_shapes=[
            pltpu.VMEM((n, tokens), F32), pltpu.VMEM((n, tokens), F32),
            pltpu.VMEM((nb, BLOCK, BLOCK), F32), pltpu.VMEM((nb, BLOCK, BLOCK), F32),
            pltpu.VMEM((n, tokens), F32), pltpu.VMEM((n, tokens), F32),
            pltpu.VMEM((heads, tokens), F32), pltpu.VMEM((heads, tokens), F32),
        ],
        compiler_params=pltpu.CompilerParams(vmem_limit_bytes=VMEM_LIMIT),
    )(
        activations, cotangent, b_proj, c_proj, rows, aux, added, inject, entry, exit_grad, alog,
        d_skip,
    )
    grad_b, grad_c = over_heads(grad_b, grad_c)
    return (grad_x, grad_b, grad_c, grad_rate)


def solution(mesh):
    tok = ("grp", "seq", "rep")
    return jax.shard_map(
        on_device,
        mesh=mesh,
        in_specs=(
            P(tok, "head"), P(tok, "head"), P(tok, None), P(tok, None), P("head", tok),
            P(tok), P(tok), P("head", None), P("head"), P("head"),
        ),
        out_specs=(P(tok, "head"), P(tok, None), P(tok, None), P("head", tok)),
        check_vma=False,
    )
```
